32 devices in a mesh: blk: 8 (over z, y), group: 4 (over x, core).
Axes of the slice: x: 2, y: 2, z: 4, core: 2. Of those that a mesh axis runs over, the one named last changes fastest.
Arguments:
- image_feats: float32 [2048, 768], P(('blk', 'group')), may hold values from -2 to 2
- text_feats: float32 [2048, 768], P(('blk', 'group')), may hold values from -2 to 2
- logit_scale: float32 [1], replicated, may hold values from 30 to 100
Outputs:
- image_grad: float32 [2048, 768], P(('blk', 'group'))
- text_grad: float32 [2048, 768], P(('blk', 'group'))
- mean_loss: float32 [1], replicated
- scale_grad: float32 [1], replicated
The draws below stay inside these ranges and needn't reach their ends.
All inputs are finite; a program needn't handle non-finite values.
Results may differ from the reference program's by a relative error of at most 0.0003.
Values sent between devices are 32-bit elements; how exact they have to be, the bound alone decides.
A program may use at most 64 MiB of HBM per device.

```python
import math
import jax
import jax.numpy as jnp
from jax import lax

E = 768
ROWS = 64
BATCH = 2048
N_GROUP = 4


def shared_texts(key):
    first = jax.random.fold_in(key, 0)
    second = jax.random.fold_in(key, 1)
    fourth = jax.random.fold_in(key, 3)
    noise = jax.random.normal(first, (BATCH, E), jnp.float32)
    base = noise / jnp.sqrt(1.0) * E ** (-0.5)
    fresh = jax.random.normal(fourth, (BATCH, E), jnp.float32) * E ** (-0.5)
    copied = jnp.sqrt(1.0) * fresh
    position = jnp.arange(BATCH)[:, None]
    base = jnp.where(position % 61 == 1, copied, base)
    widths = jnp.exp(jax.random.uniform(second, (BATCH, 1), jnp.float32, jnp.log(0.7), jnp.log(1.4)))
    return jnp.clip(base * widths, -2.0, 2.0)


def draw_text_feats(key, part):
    texts = shared_texts(key)
    return texts


def draw_image_feats(key, part):
    key = jax.random.fold_in(key, 7)
    first, second = jax.random.split(key)
    widths = jnp.exp(jax.random.uniform(second, (BATCH, 1), jnp.float32, jnp.log(0.4), jnp.log(4.0)))
    images = jax.random.normal(first, (BATCH, E), jnp.float32) * E ** (-0.5) * widths
    return jnp.clip(images, -2.0, 2.0)


def setup_inputs(seed: int = 0) -> dict:
    key_of = jax.random.split(jax.random.key(seed), 4)
    image_feats = draw_image_feats(jax.random.fold_in(key_of[3], 71), 0)
    text_feats = draw_text_feats(jax.random.fold_in(key_of[3], 71), 0)
    logit_scale = jnp.clip(jnp.exp(jax.random.uniform(key_of[2], (1,), jnp.float32, math.log(30.0), math.log(100.0))), 30.0, 100.0)
    return {"image_feats": image_feats, "text_feats": text_feats, "logit_scale": logit_scale}


def reference(image_feats, text_feats, logit_scale):
    scale = logit_scale[0]
    block = ROWS * N_GROUP
    count = BATCH // block
    image_blocks = image_feats.reshape(count, block, E)

    def scores_of(images):
        return scale * lax.dot_general(images, text_feats, (((1,), (1,)), ((), ())), precision=lax.Precision.HIGHEST)

    def forward(carry, images):
        column_top, column_total = carry
        scores = scores_of(images)
        row_top = jnp.max(scores, axis=1, keepdims=True)
        row_lse = row_top[:, 0] + jnp.log(jnp.sum(jnp.exp(scores - row_top), axis=1))
        new_top = jnp.maximum(column_top, jnp.max(scores, axis=0))
        column_total = column_total * jnp.exp(column_top - new_top) + jnp.sum(jnp.exp(scores - new_top[None, :]), axis=0)
        return (new_top, column_total), row_lse

    start = (jnp.full((BATCH,), -1e30, jnp.float32), jnp.zeros((BATCH,), jnp.float32))
    (column_top, column_total), row_blocks = lax.scan(forward, start, image_blocks)
    column_lse = column_top + jnp.log(column_total)

    def backward(carry, inputs):
        text_part, weighted = carry
        images, row_lse = inputs
        scores = scores_of(images)
        weights = 0.5 * (jnp.exp(scores - row_lse[:, None]) + jnp.exp(scores - column_lse[None, :]))
        image_part = scale * jnp.dot(weights, text_feats, precision=lax.Precision.HIGHEST)
        text_part = text_part + scale * lax.dot_general(weights, images, (((0,), (0,)), ((), ())), precision=lax.Precision.HIGHEST)
        return (text_part, weighted + jnp.sum(weights * scores)), image_part

    begin = (jnp.zeros((BATCH, E), jnp.float32), jnp.zeros((), jnp.float32))
    (text_part, weighted), image_parts = lax.scan(backward, begin, (image_blocks, row_blocks))
    image_grad = image_parts.reshape(BATCH, E) - scale * text_feats
    text_grad = text_part - scale * image_feats
    diagonal = scale * jnp.sum(image_feats * text_feats, axis=1)
    row_lse = row_blocks.reshape(BATCH)
    mean_loss = (0.5 * jnp.sum(row_lse) + 0.5 * jnp.sum(column_lse) - jnp.sum(diagonal)) / BATCH
    scale_grad = (weighted - jnp.sum(diagonal)) / (scale * BATCH)
    return image_grad, text_grad, jnp.reshape(mean_loss, (1,)), jnp.reshape(scale_grad, (1,))
```

```python
import functools

import jax
import jax.numpy as jnp
from jax import lax
from jax.experimental import pallas as pl
from jax.experimental.pallas import tpu as pltpu
from jax.sharding import PartitionSpec as P

F32 = jnp.float32
BF16 = jnp.bfloat16
MESH = pl.DeviceIdType.MESH
NT = (((1,), (1,)), ((), ()))
NN = (((1,), (0,)), ((), ()))


def dot(a, b, dims):
    return lax.dot_general(a, b, dims, preferred_element_type=F32)


def split2(x):
    hi = x.astype(BF16)
    return hi, (x - hi.astype(F32)).astype(BF16)


def split3(x):
    hi = x.astype(BF16)
    rest = x - hi.astype(F32)
    mid = rest.astype(BF16)
    return hi, mid, (rest - mid.astype(F32)).astype(BF16)


def tiles(count, fn):
    if count <= 2:
        for t in range(count):
            fn(t)
    else:
        lax.fori_loop(0, count, lambda t, c: (fn(t), c)[1], 0)


def span(t, step):
    start = t * step
    return pl.ds(start if isinstance(start, int) else pl.multiple_of(start, step), step)


def kernel(
    n_blk,
    n_group,
    width,
    scale_ref,
    image_ref,
    text_ref,
    image_grad_ref,
    text_grad_ref,
    loss_ref,
    scale_grad_ref,
    images,
    texts,
    scores,
    i_hi,
    i_mid,
    t_hi,
    t_mid,
    t_lo,
    w_hi,
    w_lo,
    wt_hi,
    wt_lo,
    part_i,
    part_t,
    from_core,
    from_y,
    from_g,
    from_x,
    from_f,
    row_stats,
    col_stats,
    totals_i,
    totals_t,
    send_sem,
    recv_sem,
):
    rows, emb = image_ref.shape
    chunks = emb // width
    n_g, n_x = n_blk // 4, n_group // 2
    half = n_blk // 2
    blk, group = lax.axis_index("blk"), lax.axis_index("group")
    f, r = blk // half, blk % half
    g, y = r // 2, r % 2
    x, core = group // 2, group % 2

    def device(f=f, g=g, y=y, x=x, core=core):
        return (f * half + g * 2 + y, x * 2 + core)

    def image_slot(g=g, y=y, core=core):
        return core * half + y * n_g + g

    def text_slot(x=x, f=f):
        return x * 2 + f

    image_peers = []
    for dc in range(2):
        for dy in range(2):
            for dg in range(n_g):
                if dc or dy or dg:
                    to = device(g=(g + dg) % n_g, y=(y + dy) % 2, core=(core + dc) % 2)
                    image_peers.append(((dg, dy, dc), ((n_g - dg) % n_g, dy, dc), to))
    text_peers = []
    for dx in range(n_x):
        for df in range(2):
            if dx or df:
                to = device(x=(x + dx) % n_x, f=(f + df) % 2)
                text_peers.append(((dx, df), ((n_x - dx) % n_x, df), to))

    barrier = pltpu.get_barrier_semaphore()
    for _, _, to in image_peers + text_peers:
        pl.semaphore_signal(barrier, inc=1, device_id=to, device_id_type=MESH)
    pl.semaphore_wait(barrier, len(image_peers) + len(text_peers))

    numbers = {}
    sent = []

    def number(name):
        return numbers.setdefault(name, len(numbers))

    def send(src, dst, to, out_name, in_name):
        copy = pltpu.make_async_remote_copy(
            src_ref=src,
            dst_ref=dst,
            send_sem=send_sem.at[number(("s",) + out_name)],
            recv_sem=recv_sem.at[number(("s",) + in_name)],
            device_id=to,
            device_id_type=MESH,
        )
        copy.start()
        sent.append(copy)

    def arrived(dst, name):
        pltpu.make_async_remote_copy(
            src_ref=dst,
            dst_ref=dst,
            send_sem=send_sem.at[number(("s",) + name)],
            recv_sem=recv_sem.at[number(("s",) + name)],
            device_id=device(core=1 - core),
            device_id_type=MESH,
        ).wait_recv()

    def cols(k):
        return pl.ds(k * width, width)

    def block(ref, slot, k, count=1):
        return ref.at[pl.ds(pl.multiple_of(slot * rows, rows), count * rows), cols(k)]

    own_i, own_t = image_slot(), text_slot()
    y2, f2, core2 = 1 - y, 1 - f, 1 - core

    for k in range(chunks):
        mine_i, mine_t = image_ref.at[:, cols(k)], text_ref.at[:, cols(k)]
        for dg in range(1, n_g):
            send(mine_i, block(images, own_i, k), device(g=(g + dg) % n_g), ("ig", dg, k), ("ig", n_g - dg, k))
        send(mine_t, block(texts, own_t, k), device(f=f2), ("tf", k), ("tf", k))
        send(mine_i, block(images, own_i, k), device(y=y2), ("iy", 0, k), ("iy", 0, k))
        for dx in range(1, n_x):
            send(mine_t, block(texts, own_t, k), device(x=(x + dx) % n_x), ("tx", dx, 0, k), ("tx", n_x - dx, 0, k))
        send(mine_i, block(images, own_i, k), device(core=core2), ("ic", 0, 0, k), ("ic", 0, 0, k))
    images[pl.ds(pl.multiple_of(own_i * rows, rows), rows), :] = image_ref[...]
    texts[pl.ds(pl.multiple_of(own_t * rows, rows), rows), :] = text_ref[...]

    def relay(k):
        for dg in range(1, n_g):
            at = block(images, image_slot(g=(g + dg) % n_g), k)
            arrived(at, ("ig", dg, k))
            send(at, at, device(y=y2), ("iy", dg, k), ("iy", dg, k))
            send(at, at, device(core=core2), ("ic", dg, 0, k), ("ic", dg, 0, k))
        at = block(texts, text_slot(f=f2), k)
        arrived(at, ("tf", k))
        for dx in range(1, n_x):
            send(at, at, device(x=(x + dx) % n_x), ("tx", dx, 1, k), ("tx", n_x - dx, 1, k))
        at = block(images, image_slot(y=y2), k)
        arrived(at, ("iy", 0, k))
        send(at, at, device(core=core2), ("ic", 0, 1, k), ("ic", 0, 1, k))

    def relay_last(k):
        for dg in range(1, n_g):
            at = block(images, image_slot(g=(g + dg) % n_g, y=y2), k)
            arrived(at, ("iy", dg, k))
            send(at, at, device(core=core2), ("ic", dg, 1, k), ("ic", dg, 1, k))

    def collect(k):
        for dx in range(1, n_x):
            for df in range(2):
                arrived(block(texts, text_slot(x=(x + dx) % n_x, f=(f + df) % 2), k), ("tx", dx, df, k))
        for dg in range(n_g):
            for dy in range(2):
                at = block(images, image_slot(g=(g + dg) % n_g, y=(y + dy) % 2, core=core2), k)
                arrived(at, ("ic", dg, dy, k))

    scale = scale_ref[0]
    n_images, n_texts = images.shape[0], texts.shape[0]
    step = min(256, n_images)
    steps = n_images // step

    def score(k):
        col = cols(k)
        hi, mid, lo = split3(texts[:, col])
        t_hi[:, col], t_mid[:, col], t_lo[...] = hi, mid, lo

        def tile(t):
            part = span(t, step)
            a_hi, a_mid, a_lo = split3(images[part, col])
            i_hi[part, col], i_mid[part, col] = a_hi, a_mid
            b_hi, b_mid, b_lo = t_hi[:, col], t_mid[:, col], t_lo[...]
            total = dot(a_lo, b_hi, NT) + dot(a_hi, b_lo, NT) + dot(a_mid, b_mid, NT)
            total = total + dot(a_mid, b_hi, NT) + dot(a_hi, b_mid, NT)
            total = total + dot(a_hi, b_hi, NT)
            if k > 0:
                total = total + scores[part, :]
            if k == chunks - 1:
                total = scale * total
            scores[part, :] = total

        tiles(steps, tile)

    relay(0)
    for k in range(chunks):
        relay_last(k)
        if k + 1 < chunks:
            relay(k + 1)
        collect(k)
        score(k)

    def to_lanes(column):
        return jnp.transpose(jnp.broadcast_to(column, (column.shape[0], 128)))[0:1, :]

    def to_rows(line):
        return jnp.transpose(jnp.broadcast_to(line, (128, line.shape[1])))[:, 0:1]

    col_stats[own_t] = jnp.full((1, n_texts), -3e38, F32)

    def row_tile(t):
        part = span(t, step)
        s = scores[part, :]
        top = jnp.max(s, axis=1, keepdims=True)
        total = jnp.sum(jnp.exp(s - top), axis=1, keepdims=True)
        row_stats[own_i, :, part] = to_lanes(top + jnp.log(total))
        col_stats[own_t] = jnp.maximum(col_stats[own_t], jnp.max(s, axis=0, keepdims=True))

    tiles(steps, row_tile)
    for (dg, dy, dc), back, to in image_peers:
        here = row_stats.at[own_i]
        send(here, here, to, ("rs", dg, dy, dc), ("rs",) + back)

    col_top = col_stats[own_t]
    col_stats[own_t] = jnp.zeros((1, n_texts), F32)

    def col_tile(t):
        s = scores[span(t, step), :]
        col_stats[own_t] = col_stats[own_t] + jnp.sum(jnp.exp(s - col_top), axis=0, keepdims=True)

    tiles(steps, col_tile)
    col_stats[own_t] = col_top + jnp.log(col_stats[own_t])
    for (dx, df), back, to in text_peers:
        here = col_stats.at[own_t]
        send(here, here, to, ("cs", dx, df), ("cs",) + back)

    diagonal = scale * jnp.sum(image_ref[...] * text_ref[...])

    for (dg, dy, dc), _, _ in image_peers:
        slot = image_slot((g + dg) % n_g, (y + dy) % 2, (core + dc) % 2)
        arrived(row_stats.at[slot], ("rs", dg, dy, dc))
    for (dx, df), _, _ in text_peers:
        arrived(col_stats.at[text_slot((x + dx) % n_x, (f + df) % 2)], ("cs", dx, df))

    def merged(stats):
        every = stats[...]
        top = jnp.max(every, axis=0)
        return top + jnp.log(jnp.sum(jnp.exp(every - top[None]), axis=0))

    row_lse, col_lse = merged(row_stats), merged(col_stats)

    weighted = jnp.zeros((1, n_texts), F32)
    for t in range(steps):
        part = span(t, step)
        s = scores[part, :]
        w = 0.5 * (jnp.exp(s - to_rows(row_lse[:, t * step : (t + 1) * step])) + jnp.exp(s - col_lse))
        weighted = weighted + jnp.sum(w * s, axis=0, keepdims=True)
        w_hi[part, :], w_lo[part, :] = split2(w)
        wt_hi[:, part], wt_lo[:, part] = split2(jnp.transpose(w))

    t_step = min(256, n_texts)

    def partial_texts(k):
        col = cols(k)

        def tile(t):
            part = span(t, t_step)
            a_hi, a_lo, b_hi, b_lo = wt_hi[part, :], wt_lo[part, :], i_hi[:, col], i_mid[:, col]
            part_t[part, col] = dot(a_lo, b_hi, NN) + dot(a_hi, b_lo, NN) + dot(a_hi, b_hi, NN)

        tiles(n_texts // t_step, tile)

    def partial_images(k):
        col = cols(k)

        def tile(t):
            part = span(t, step)
            a_hi, a_lo, b_hi, b_lo = w_hi[part, :], w_lo[part, :], t_hi[:, col], t_mid[:, col]
            part_i[part, col] = dot(a_lo, b_hi, NN) + dot(a_hi, b_lo, NN) + dot(a_hi, b_hi, NN)

        tiles(steps, tile)

    for k in range(chunks):
        partial_images(k)
        send(block(part_i, core2 * half, k, half), from_core.at[:, cols(k)], device(core=core2), ("bc", k), ("bc", k))
        partial_texts(k)
        for dx in range(1, n_x):
            xx = (x + dx) % n_x
            src, dst = block(part_t, xx * 2, k, 2), from_x.at[n_x - dx - 1, :, cols(k)]
            send(src, dst, device(x=xx), ("bx", dx, k), ("bx", n_x - dx, k))

    row_lane = lax.broadcasted_iota(jnp.int32, (1, n_images), 1) // rows
    col_lane = lax.broadcasted_iota(jnp.int32, (1, n_texts), 1) // rows
    own_rows = jnp.sum(jnp.where(row_lane == own_i, row_lse, 0.0))
    own_cols = jnp.sum(jnp.where(col_lane == own_t, col_lse, 0.0))
    loss_part = 0.5 * own_rows + 0.5 * own_cols - diagonal
    scale_part = jnp.sum(weighted) - diagonal
    lane = lax.broadcasted_iota(jnp.int32, (1, 128), 1)
    totals_i[own_i] = jnp.where(lane == 0, loss_part, jnp.where(lane == 1, scale_part, 0.0))
    for (dg, dy, dc), back, to in image_peers:
        here = totals_i.at[own_i]
        send(here, here, to, ("ti", dg, dy, dc), ("ti",) + back)

    def rows_of(slot, count=1):
        return pl.ds(pl.multiple_of(slot * rows, rows), count * rows)

    base = core * half
    for k in range(chunks):
        col = cols(k)
        arrived(from_core.at[:, col], ("bc", k))
        away = rows_of(base + y2 * n_g, n_g)
        part_i[away, col] = part_i[away, col] + from_core[rows_of(y2 * n_g, n_g), col]
        send(part_i.at[away, col], from_y.at[:, col], device(y=y2), ("by", k), ("by", k))
        keep = rows_of(base + y * n_g, n_g)
        part_i[keep, col] = part_i[keep, col] + from_core[rows_of(y * n_g, n_g), col]

    for k in range(chunks):
        col = cols(k)
        for dx in range(1, n_x):
            arrived(from_x.at[dx - 1, :, col], ("bx", dx, k))
        away, keep = rows_of(x * 2 + f2), rows_of(x * 2 + f)
        total_away, total_keep = part_t[away, col], part_t[keep, col]
        for dx in range(1, n_x):
            total_away = total_away + from_x[dx - 1, rows_of(f2), col]
            total_keep = total_keep + from_x[dx - 1, rows_of(f), col]
        part_t[away, col] = total_away
        send(part_t.at[away, col], from_f.at[:, col], device(f=f2), ("bf", k), ("bf", k))
        part_t[keep, col] = total_keep

        arrived(from_y.at[:, col], ("by", k))
        for dg in range(1, n_g):
            gg = (g + dg) % n_g
            away = rows_of(base + y * n_g + gg)
            part_i[away, col] = part_i[away, col] + from_y[rows_of(gg), col]
            dst = from_g.at[n_g - dg - 1, :, col]
            send(part_i.at[away, col], dst, device(g=gg), ("bg", dg, k), ("bg", n_g - dg, k))

    for (dg, dy, dc), _, _ in image_peers:
        slot = image_slot((g + dg) % n_g, (y + dy) % 2, (core + dc) % 2)
        arrived(totals_i.at[slot], ("ti", dg, dy, dc))
    totals_t[own_t] = jnp.sum(totals_i[...], axis=0)
    for (dx, df), back, to in text_peers:
        here = totals_t.at[own_t]
        send(here, here, to, ("tt", dx, df), ("tt",) + back)

    for k in range(chunks):
        col = cols(k)
        arrived(from_f.at[:, col], ("bf", k))
        total = part_t[rows_of(x * 2 + f), col] + from_f[:, col]
        text_grad_ref[:, col] = scale * (total - image_ref[:, col])
        total = part_i[rows_of(own_i), col] + from_y[rows_of(g), col]
        for dg in range(1, n_g):
            arrived(from_g.at[dg - 1, :, col], ("bg", dg, k))
            total = total + from_g[dg - 1, :, col]
        image_grad_ref[:, col] = scale * (total - text_ref[:, col])

    for (dx, df), _, _ in text_peers:
        arrived(totals_t.at[text_slot((x + dx) % n_x, (f + df) % 2)], ("tt", dx, df))
    total = jnp.sum(totals_t[...], axis=0)
    batch = rows * n_blk * n_group
    loss_ref[0] = jnp.sum(jnp.where(lane == 0, total, 0.0)) / batch
    scale_grad_ref[0] = jnp.sum(jnp.where(lane == 1, total, 0.0)) / (scale * batch)

    for copy in sent:
        copy.wait_send()


def body(n_blk, n_group, image_feats, text_feats, logit_scale):
    rows, emb = image_feats.shape
    width = 256 if emb % 256 == 0 else emb
    chunks = emb // width
    n_g, n_x = n_blk // 4, n_group // 2
    n_images, n_texts = rows * n_blk, rows * n_group
    count = chunks * (n_g * 4 + n_x * 4 + 8) + 2 * (n_blk + n_group)
    vmem = pl.BlockSpec(memory_space=pltpu.VMEM)
    smem = pl.BlockSpec(memory_space=pltpu.SMEM)
    image_grad, text_grad, mean_loss, scale_grad = pl.pallas_call(
        functools.partial(kernel, n_blk, n_group, width),
        out_shape=(
            jax.ShapeDtypeStruct((rows, emb), F32),
            jax.ShapeDtypeStruct((rows, emb), F32),
            jax.ShapeDtypeStruct((1,), F32),
            jax.ShapeDtypeStruct((1,), F32),
        ),
        in_specs=[smem, vmem, vmem],
        out_specs=(vmem, vmem, smem, smem),
        scratch_shapes=[
            pltpu.VMEM((n_images, emb), F32),
            pltpu.VMEM((n_texts, emb), F32),
            pltpu.VMEM((n_images, n_texts), F32),
            pltpu.VMEM((n_images, emb), BF16),
            pltpu.VMEM((n_images, emb), BF16),
            pltpu.VMEM((n_texts, emb), BF16),
            pltpu.VMEM((n_texts, emb), BF16),
            pltpu.VMEM((n_texts, width), BF16),
            pltpu.VMEM((n_images, n_texts), BF16),
            pltpu.VMEM((n_images, n_texts), BF16),
            pltpu.VMEM((n_texts, n_images), BF16),
            pltpu.VMEM((n_texts, n_images), BF16),
            pltpu.VMEM((n_images, emb), F32),
            pltpu.VMEM((n_texts, emb), F32),
            pltpu.VMEM((n_images // 2, emb), F32),
            pltpu.VMEM((n_g * rows, emb), F32),
            pltpu.VMEM((max(n_g - 1, 1), rows, emb), F32),
            pltpu.VMEM((max(n_x - 1, 1), 2 * rows, emb), F32),
            pltpu.VMEM((rows, emb), F32),
            pltpu.VMEM((n_blk, 1, n_images), F32),
            pltpu.VMEM((n_group, 1, n_texts), F32),
            pltpu.VMEM((n_blk, 1, 128), F32),
            pltpu.VMEM((n_group, 1, 128), F32),
            pltpu.SemaphoreType.DMA((count,)),
            pltpu.SemaphoreType.DMA((count,)),
        ],
        compiler_params=pltpu.CompilerParams(
            collective_id=0, has_side_effects=True, vmem_limit_bytes=56 * 1024 * 1024
        ),
        name="contrastive",
    )(logit_scale, image_feats, text_feats)
    return image_grad, text_grad, mean_loss, scale_grad


def solution(mesh):
    return jax.shard_map(
        functools.partial(body, mesh.shape["blk"], mesh.shape["group"]),
        mesh=mesh,
        in_specs=(P(("blk", "group"), None), P(("blk", "group"), None), P()),
        out_specs=(P(("blk", "group"), None), P(("blk", "group"), None), P(), P()),
        check_vma=False,
    )
```

```python
import functools

import jax
import jax.numpy as jnp
from jax import lax
from jax.experimental import pallas as pl
from jax.experimental.pallas import tpu as pltpu
from jax.sharding import PartitionSpec as P

F32 = jnp.float32
BF16 = jnp.bfloat16
MESH = pl.DeviceIdType.MESH
NT = (((1,), (1,)), ((), ()))
NN = (((1,), (0,)), ((), ()))


LINK_WIDTH = 256
AHEAD = 2
BACK_AHEAD = 2


def dot(a, b, dims):
    return lax.dot_general(a, b, dims, preferred_element_type=F32)


def split2(x):
    hi = x.astype(BF16)
    return hi, (x - hi.astype(F32)).astype(BF16)


def split3(x):
    hi = x.astype(BF16)
    rest = x - hi.astype(F32)
    mid = rest.astype(BF16)
    return hi, mid, (rest - mid.astype(F32)).astype(BF16)


def tiles(count, fn):
    if count <= 2:
        for t in range(count):
            fn(t)
    else:
        lax.fori_loop(0, count, lambda t, c: (fn(t), c)[1], 0)


def span(t, step):
    start = t * step
    return pl.ds(start if isinstance(start, int) else pl.multiple_of(start, step), step)


def kernel(
    n_blk,
    n_group,
    width,
    scale_ref,
    image_ref,
    text_ref,
    image_grad_ref,
    text_grad_ref,
    loss_ref,
    scale_grad_ref,
    images,
    texts,
    scores,
    i_hi,
    i_mid,
    t_hi,
    t_mid,
    t_lo,
    w_hi,
    w_lo,
    wt_hi,
    wt_lo,
    part_i,
    part_t,
    from_core,
    from_y,
    from_g,
    from_x,
    from_f,
    row_stats,
    col_stats,
    totals_i,
    totals_t,
    send_sem,
    recv_sem,
):
    rows, emb = image_ref.shape
    chunks = emb // width
    link = LINK_WIDTH if width % LINK_WIDTH == 0 else width
    links, ratio = emb // link, width // link
    n_g, n_x = n_blk // 4, n_group // 2
    half = n_blk // 2
    blk, group = lax.axis_index("blk"), lax.axis_index("group")
    f, r = blk // half, blk % half
    g, y = r // 2, r % 2
    x, core = group // 2, group % 2

    def device(f=f, g=g, y=y, x=x, core=core):
        return (f * half + g * 2 + y, x * 2 + core)

    def image_slot(g=g, y=y, core=core):
        return core * half + y * n_g + g

    def text_slot(x=x, f=f):
        return x * 2 + f

    image_peers = []
    for dc in range(2):
        for dy in range(2):
            for dg in range(n_g):
                if dc or dy or dg:
                    to = device(g=(g + dg) % n_g, y=(y + dy) % 2, core=(core + dc) % 2)
                    image_peers.append(((dg, dy, dc), ((n_g - dg) % n_g, dy, dc), to))
    text_peers = []
    for dx in range(n_x):
        for df in range(2):
            if dx or df:
                to = device(x=(x + dx) % n_x, f=(f + df) % 2)
                text_peers.append(((dx, df), ((n_x - dx) % n_x, df), to))

    barrier = pltpu.get_barrier_semaphore()
    for _, _, to in image_peers + text_peers:
        pl.semaphore_signal(barrier, inc=1, device_id=to, device_id_type=MESH)
    pl.semaphore_wait(barrier, len(image_peers) + len(text_peers))

    numbers = {}
    sent = []

    def number(name):
        return numbers.setdefault(name, len(numbers))

    def send(src, dst, to, out_name, in_name):
        copy = pltpu.make_async_remote_copy(
            src_ref=src,
            dst_ref=dst,
            send_sem=send_sem.at[number(("s",) + out_name)],
            recv_sem=recv_sem.at[number(("s",) + in_name)],
            device_id=to,
            device_id_type=MESH,
        )
        copy.start()
        sent.append(copy)

    def arrived(dst, name):
        pltpu.make_async_remote_copy(
            src_ref=dst,
            dst_ref=dst,
            send_sem=send_sem.at[number(("s",) + name)],
            recv_sem=recv_sem.at[number(("s",) + name)],
            device_id=device(core=1 - core),
            device_id_type=MESH,
        ).wait_recv()

    def cols(k):
        return pl.ds(k * width, width)

    def lcols(k):
        return pl.ds(k * link, link)

    def block(ref, slot, k, count=1):
        return ref.at[pl.ds(pl.multiple_of(slot * rows, rows), count * rows), lcols(k)]

    own_i, own_t = image_slot(), text_slot()
    y2, f2, core2 = 1 - y, 1 - f, 1 - core

    def begin(k):
        mine_i, mine_t = image_ref.at[:, lcols(k)], text_ref.at[:, lcols(k)]
        send(mine_t, block(texts, own_t, k), device(f=f2), ("tf", k), ("tf", k))
        for dg in range(1, n_g):
            send(mine_i, block(images, own_i, k), device(g=(g + dg) % n_g), ("ig", dg, k), ("ig", n_g - dg, k))
        send(mine_i, block(images, own_i, k), device(y=y2), ("iy", 0, k), ("iy", 0, k))
        for dx in range(1, n_x):
            send(mine_t, block(texts, own_t, k), device(x=(x + dx) % n_x), ("tx", dx, 0, k), ("tx", n_x - dx, 0, k))
        send(mine_i, block(images, own_i, k), device(core=core2), ("ic", 0, 0, k), ("ic", 0, 0, k))

    ahead = min(AHEAD, links)
    for k in range(ahead):
        begin(k)
    images[pl.ds(pl.multiple_of(own_i * rows, rows), rows), :] = image_ref[...]
    texts[pl.ds(pl.multiple_of(own_t * rows, rows), rows), :] = text_ref[...]

    def relay(k):
        for dg in range(1, n_g):
            at = block(images, image_slot(g=(g + dg) % n_g), k)
            arrived(at, ("ig", dg, k))
            send(at, at, device(y=y2), ("iy", dg, k), ("iy", dg, k))
            send(at, at, device(core=core2), ("ic", dg, 0, k), ("ic", dg, 0, k))
        at = block(texts, text_slot(f=f2), k)
        arrived(at, ("tf", k))
        for dx in range(1, n_x):
            send(at, at, device(x=(x + dx) % n_x), ("tx", dx, 1, k), ("tx", n_x - dx, 1, k))
        at = block(images, image_slot(y=y2), k)
        arrived(at, ("iy", 0, k))
        send(at, at, device(core=core2), ("ic", 0, 1, k), ("ic", 0, 1, k))

    def relay_last(k):
        for dg in range(1, n_g):
            at = block(images, image_slot(g=(g + dg) % n_g, y=y2), k)
            arrived(at, ("iy", dg, k))
            send(at, at, device(core=core2), ("ic", dg, 1, k), ("ic", dg, 1, k))

    def collect(k):
        for dx in range(1, n_x):
            for df in range(2):
                arrived(block(texts, text_slot(x=(x + dx) % n_x, f=(f + df) % 2), k), ("tx", dx, df, k))
        for dg in range(n_g):
            for dy in range(2):
                at = block(images, image_slot(g=(g + dg) % n_g, y=(y + dy) % 2, core=core2), k)
                arrived(at, ("ic", dg, dy, k))

    scale = scale_ref[0]
    n_images, n_texts = images.shape[0], texts.shape[0]
    step = min(256, n_images)
    steps = n_images // step

    def score(k):
        col = cols(k)
        hi, mid, lo = split3(texts[:, col])
        t_hi[:, col], t_mid[:, col], t_lo[...] = hi, mid, lo

        def tile(t):
            part = span(t, step)
            a_hi, a_mid, a_lo = split3(images[part, col])
            i_hi[part, col], i_mid[part, col] = a_hi, a_mid
            b_hi, b_mid, b_lo = t_hi[:, col], t_mid[:, col], t_lo[...]
            total = dot(a_lo, b_hi, NT) + dot(a_hi, b_lo, NT) + dot(a_mid, b_mid, NT)
            total = total + dot(a_mid, b_hi, NT) + dot(a_hi, b_mid, NT)
            total = total + dot(a_hi, b_hi, NT)
            if k > 0:
                total = total + scores[part, :]
            if k == chunks - 1:
                total = scale * total
            scores[part, :] = total

        tiles(steps, tile)

    for k in range(links + 2):
        if k < links:
            relay(k)
        if k + ahead < links:
            begin(k + ahead)
        if 1 <= k <= links:
            relay_last(k - 1)
        if k >= 2:
            collect(k - 2)
            if (k - 1) % ratio == 0:
                score((k - 1) // ratio - 1)

    def to_lanes(column):
        return jnp.transpose(jnp.broadcast_to(column, (column.shape[0], 128)))[0:1, :]

    def to_rows(line):
        return jnp.transpose(jnp.broadcast_to(line, (128, line.shape[1])))[:, 0:1]

    col_stats[own_t] = jnp.full((1, n_texts), -3e38, F32)

    def row_tile(t):
        part = span(t, step)
        s = scores[part, :]
        top = jnp.max(s, axis=1, keepdims=True)
        total = jnp.sum(jnp.exp(s - top), axis=1, keepdims=True)
        row_stats[own_i, :, part] = to_lanes(top + jnp.log(total))
        col_stats[own_t] = jnp.maximum(col_stats[own_t], jnp.max(s, axis=0, keepdims=True))

    tiles(steps, row_tile)
    for (dg, dy, dc), back, to in image_peers:
        here = row_stats.at[own_i]
        send(here, here, to, ("rs", dg, dy, dc), ("rs",) + back)

    col_top = col_stats[own_t]
    col_stats[own_t] = jnp.zeros((1, n_texts), F32)

    def col_tile(t):
        s = scores[span(t, step), :]
        col_stats[own_t] = col_stats[own_t] + jnp.sum(jnp.exp(s - col_top), axis=0, keepdims=True)

    tiles(steps, col_tile)
    col_stats[own_t] = col_top + jnp.log(col_stats[own_t])
    for (dx, df), back, to in text_peers:
        here = col_stats.at[own_t]
        send(here, here, to, ("cs", dx, df), ("cs",) + back)

    diagonal = scale * jnp.sum(image_ref[...] * text_ref[...])

    for (dg, dy, dc), _, _ in image_peers:
        slot = image_slot((g + dg) % n_g, (y + dy) % 2, (core + dc) % 2)
        arrived(row_stats.at[slot], ("rs", dg, dy, dc))
    for (dx, df), _, _ in text_peers:
        arrived(col_stats.at[text_slot((x + dx) % n_x, (f + df) % 2)], ("cs", dx, df))

    def merged(stats):
        every = stats[...]
        top = jnp.max(every, axis=0)
        return top + jnp.log(jnp.sum(jnp.exp(every - top[None]), axis=0))

    row_lse, col_lse = merged(row_stats), merged(col_stats)

    weighted = jnp.zeros((1, n_texts), F32)
    for t in range(steps):
        part = span(t, step)
        s = scores[part, :]
        w = 0.5 * (jnp.exp(s - to_rows(row_lse[:, t * step : (t + 1) * step])) + jnp.exp(s - col_lse))
        weighted = weighted + jnp.sum(w * s, axis=0, keepdims=True)
        w_hi[part, :], w_lo[part, :] = split2(w)
        wt_hi[:, part], wt_lo[:, part] = split2(jnp.transpose(w))

    t_step = min(256, n_texts)

    def partial_texts(k):
        col = cols(k)

        def tile(t):
            part = span(t, t_step)
            a_hi, a_lo, b_hi, b_lo = wt_hi[part, :], wt_lo[part, :], i_hi[:, col], i_mid[:, col]
            part_t[part, col] = dot(a_lo, b_hi, NN) + dot(a_hi, b_lo, NN) + dot(a_hi, b_hi, NN)

        tiles(n_texts // t_step, tile)

    def partial_images(k):
        col = cols(k)

        def tile(t):
            part = span(t, step)
            a_hi, a_lo, b_hi, b_lo = w_hi[part, :], w_lo[part, :], t_hi[:, col], t_mid[:, col]
            part_i[part, col] = dot(a_lo, b_hi, NN) + dot(a_hi, b_lo, NN) + dot(a_hi, b_hi, NN)

        tiles(steps, tile)

    def rows_of(slot, count=1):
        return pl.ds(pl.multiple_of(slot * rows, rows), count * rows)

    def send_x(k):
        for dx in range(1, n_x):
            xx = (x + dx) % n_x
            src, dst = block(part_t, xx * 2, k, 2), from_x.at[n_x - dx - 1, :, lcols(k)]
            send(src, dst, device(x=xx), ("bx", dx, k), ("bx", n_x - dx, k))

    def send_core(k):
        src, dst = block(part_i, core2 * half, k, half), from_core.at[:, lcols(k)]
        send(src, dst, device(core=core2), ("bc", k), ("bc", k))

    base = core * half

    def send_y(k):
        col = lcols(k)
        arrived(from_core.at[:, col], ("bc", k))
        away = rows_of(base + y2 * n_g, n_g)
        part_i[away, col] = part_i[away, col] + from_core[rows_of(y2 * n_g, n_g), col]
        send(part_i.at[away, col], from_y.at[:, col], device(y=y2), ("by", k), ("by", k))
        keep = rows_of(base + y * n_g, n_g)
        part_i[keep, col] = part_i[keep, col] + from_core[rows_of(y * n_g, n_g), col]

    def send_f(k):
        col = lcols(k)
        for dx in range(1, n_x):
            arrived(from_x.at[dx - 1, :, col], ("bx", dx, k))
        away, keep = rows_of(x * 2 + f2), rows_of(x * 2 + f)
        total = part_t[away, col]
        for dx in range(1, n_x):
            total = total + from_x[dx - 1, rows_of(f2), col]
        part_t[away, col] = total
        send(part_t.at[away, col], from_f.at[:, col], device(f=f2), ("bf", k), ("bf", k))
        total = part_t[keep, col]
        for dx in range(1, n_x):
            total = total + from_x[dx - 1, rows_of(f), col]
        part_t[keep, col] = total

    def send_g(k):
        col = lcols(k)
        arrived(from_y.at[:, col], ("by", k))
        for dg in range(1, n_g):
            gg = (g + dg) % n_g
            away = rows_of(base + y * n_g + gg)
            part_i[away, col] = part_i[away, col] + from_y[rows_of(gg), col]
            dst = from_g.at[n_g - dg - 1, :, col]
            send(part_i.at[away, col], dst, device(g=gg), ("bg", dg, k), ("bg", n_g - dg, k))

    behind = min(BACK_AHEAD, links)
    for k in range(chunks):
        partial_texts(k)
        for j in range(k * ratio, (k + 1) * ratio):
            if j < behind:
                send_x(j)
        partial_images(k)
        for j in range(k * ratio, (k + 1) * ratio):
            send_core(j)
            if j < behind:
                send_y(j)

    row_lane = lax.broadcasted_iota(jnp.int32, (1, n_images), 1) // rows
    col_lane = lax.broadcasted_iota(jnp.int32, (1, n_texts), 1) // rows
    own_rows = jnp.sum(jnp.where(row_lane == own_i, row_lse, 0.0))
    own_cols = jnp.sum(jnp.where(col_lane == own_t, col_lse, 0.0))
    loss_part = 0.5 * own_rows + 0.5 * own_cols - diagonal
    scale_part = jnp.sum(weighted) - diagonal
    lane = lax.broadcasted_iota(jnp.int32, (1, 128), 1)
    totals_i[own_i] = jnp.where(lane == 0, loss_part, jnp.where(lane == 1, scale_part, 0.0))
    for (dg, dy, dc), back, to in image_peers:
        here = totals_i.at[own_i]
        send(here, here, to, ("ti", dg, dy, dc), ("ti",) + back)

    for k in range(links):
        send_f(k)
        if k + behind < links:
            send_x(k + behind)
        send_g(k)
        if k + behind < links:
            send_y(k + behind)

    for (dg, dy, dc), _, _ in image_peers:
        slot = image_slot((g + dg) % n_g, (y + dy) % 2, (core + dc) % 2)
        arrived(totals_i.at[slot], ("ti", dg, dy, dc))
    totals_t[own_t] = jnp.sum(totals_i[...], axis=0)
    for (dx, df), back, to in text_peers:
        here = totals_t.at[own_t]
        send(here, here, to, ("tt", dx, df), ("tt",) + back)

    for k in range(links):
        col = lcols(k)
        arrived(from_f.at[:, col], ("bf", k))
        total = part_t[rows_of(x * 2 + f), col] + from_f[:, col]
        text_grad_ref[:, col] = scale * (total - image_ref[:, col])
        total = part_i[rows_of(own_i), col] + from_y[rows_of(g), col]
        for dg in range(1, n_g):
            arrived(from_g.at[dg - 1, :, col], ("bg", dg, k))
            total = total + from_g[dg - 1, :, col]
        image_grad_ref[:, col] = scale * (total - text_ref[:, col])

    for (dx, df), _, _ in text_peers:
        arrived(totals_t.at[text_slot((x + dx) % n_x, (f + df) % 2)], ("tt", dx, df))
    total = jnp.sum(totals_t[...], axis=0)
    batch = rows * n_blk * n_group
    loss_ref[0] = jnp.sum(jnp.where(lane == 0, total, 0.0)) / batch
    scale_grad_ref[0] = jnp.sum(jnp.where(lane == 1, total, 0.0)) / (scale * batch)

    for copy in sent:
        copy.wait_send()


def body(n_blk, n_group, image_feats, text_feats, logit_scale):
    rows, emb = image_feats.shape
    width = 256 if emb % 256 == 0 else emb
    n_g, n_x = n_blk // 4, n_group // 2
    n_images, n_texts = rows * n_blk, rows * n_group
    links = emb // (LINK_WIDTH if width % LINK_WIDTH == 0 else width)
    count = links * (n_g * 4 + n_x * 4 + 8) + 2 * (n_blk + n_group)
    vmem = pl.BlockSpec(memory_space=pltpu.VMEM)
    smem = pl.BlockSpec(memory_space=pltpu.SMEM)
    image_grad, text_grad, mean_loss, scale_grad = pl.pallas_call(
        functools.partial(kernel, n_blk, n_group, width),
        out_shape=(
            jax.ShapeDtypeStruct((rows, emb), F32),
            jax.ShapeDtypeStruct((rows, emb), F32),
            jax.ShapeDtypeStruct((1,), F32),
            jax.ShapeDtypeStruct((1,), F32),
        ),
        in_specs=[smem, vmem, vmem],
        out_specs=(vmem, vmem, smem, smem),
        scratch_shapes=[
            pltpu.VMEM((n_images, emb), F32),
            pltpu.VMEM((n_texts, emb), F32),
            pltpu.VMEM((n_images, n_texts), F32),
            pltpu.VMEM((n_images, emb), BF16),
            pltpu.VMEM((n_images, emb), BF16),
            pltpu.VMEM((n_texts, emb), BF16),
            pltpu.VMEM((n_texts, emb), BF16),
            pltpu.VMEM((n_texts, width), BF16),
            pltpu.VMEM((n_images, n_texts), BF16),
            pltpu.VMEM((n_images, n_texts), BF16),
            pltpu.VMEM((n_texts, n_images), BF16),
            pltpu.VMEM((n_texts, n_images), BF16),
            pltpu.VMEM((n_images, emb), F32),
            pltpu.VMEM((n_texts, emb), F32),
            pltpu.VMEM((n_images // 2, emb), F32),
            pltpu.VMEM((n_g * rows, emb), F32),
            pltpu.VMEM((max(n_g - 1, 1), rows, emb), F32),
            pltpu.VMEM((max(n_x - 1, 1), 2 * rows, emb), F32),
            pltpu.VMEM((rows, emb), F32),
            pltpu.VMEM((n_blk, 1, n_images), F32),
            pltpu.VMEM((n_group, 1, n_texts), F32),
            pltpu.VMEM((n_blk, 1, 128), F32),
            pltpu.VMEM((n_group, 1, 128), F32),
            pltpu.SemaphoreType.DMA((count,)),
            pltpu.SemaphoreType.DMA((count,)),
        ],
        compiler_params=pltpu.CompilerParams(
            collective_id=0, has_side_effects=True, vmem_limit_bytes=56 * 1024 * 1024
        ),
        name="contrastive",
    )(logit_scale, image_feats, text_feats)
    return image_grad, text_grad, mean_loss, scale_grad


def solution(mesh):
    return jax.shard_map(
        functools.partial(body, mesh.shape["blk"], mesh.shape["group"]),
        mesh=mesh,
        in_specs=(P(("blk", "group"), None), P(("blk", "group"), None), P()),
        out_specs=(P(("blk", "group"), None), P(("blk", "group"), None), P(), P()),
        check_vma=False,
    )
```

```python
import functools

import jax
import jax.numpy as jnp
from jax import lax
from jax.experimental import pallas as pl
from jax.experimental.pallas import tpu as pltpu
from jax.sharding import PartitionSpec as P

F32 = jnp.float32
BF16 = jnp.bfloat16
MESH = pl.DeviceIdType.MESH
NT = (((1,), (1,)), ((), ()))
NN = (((1,), (0,)), ((), ()))


LINK_WIDTH = 256
AHEAD = 2
EARLY = 1


def dot(a, b, dims):
    return lax.dot_general(a, b, dims, preferred_element_type=F32)


def split2(x):
    hi = x.astype(BF16)
    return hi, (x - hi.astype(F32)).astype(BF16)


def split3(x):
    hi = x.astype(BF16)
    rest = x - hi.astype(F32)
    mid = rest.astype(BF16)
    return hi, mid, (rest - mid.astype(F32)).astype(BF16)


def tiles(count, fn):
    if count <= 2:
        for t in range(count):
            fn(t)
    else:
        lax.fori_loop(0, count, lambda t, c: (fn(t), c)[1], 0)


def span(t, step):
    start = t * step
    return pl.ds(start if isinstance(start, int) else pl.multiple_of(start, step), step)


def kernel(
    n_blk,
    n_group,
    width,
    scale_ref,
    image_ref,
    text_ref,
    image_grad_ref,
    text_grad_ref,
    loss_ref,
    scale_grad_ref,
    images,
    texts,
    scores,
    i_hi,
    i_mid,
    t_hi,
    t_mid,
    t_lo,
    w_hi,
    w_lo,
    wt_hi,
    wt_lo,
    part_i,
    part_t,
    from_core,
    from_y,
    from_g,
    from_x,
    from_f,
    row_stats,
    col_stats,
    totals_i,
    totals_t,
    send_sem,
    recv_sem,
    load_sem,
):
    rows, emb = image_ref.shape
    chunks = emb // width
    link = LINK_WIDTH if width % LINK_WIDTH == 0 else width
    links, ratio = emb // link, width // link
    n_g, n_x = n_blk // 4, n_group // 2
    half = n_blk // 2
    blk, group = lax.axis_index("blk"), lax.axis_index("group")
    f, r = blk // half, blk % half
    g, y = r // 2, r % 2
    x, core = group // 2, group % 2

    def device(f=f, g=g, y=y, x=x, core=core):
        return (f * half + g * 2 + y, x * 2 + core)

    def image_slot(g=g, y=y, core=core):
        return core * half + y * n_g + g

    def text_slot(x=x, f=f):
        return x * 2 + f

    image_peers = []
    for dc in range(2):
        for dy in range(2):
            for dg in range(n_g):
                if dc or dy or dg:
                    to = device(g=(g + dg) % n_g, y=(y + dy) % 2, core=(core + dc) % 2)
                    image_peers.append(((dg, dy, dc), ((n_g - dg) % n_g, dy, dc), to))
    text_peers = []
    for dx in range(n_x):
        for df in range(2):
            if dx or df:
                to = device(x=(x + dx) % n_x, f=(f + df) % 2)
                text_peers.append(((dx, df), ((n_x - dx) % n_x, df), to))

    own_i, own_t = image_slot(), text_slot()
    own_images = pl.ds(pl.multiple_of(own_i * rows, rows), rows)
    own_texts = pl.ds(pl.multiple_of(own_t * rows, rows), rows)
    loads = [
        pltpu.make_async_copy(image_ref, images.at[own_images], load_sem.at[0]),
        pltpu.make_async_copy(text_ref, texts.at[own_texts], load_sem.at[1]),
    ]
    barrier = pltpu.get_barrier_semaphore()
    for _, _, to in text_peers + image_peers:
        pl.semaphore_signal(barrier, inc=1, device_id=to, device_id_type=MESH)
    for load in loads:
        load.start()
    pl.semaphore_wait(barrier, len(image_peers) + len(text_peers))
    for load in loads:
        load.wait()

    numbers = {}
    sent = []

    def number(name):
        return numbers.setdefault(name, len(numbers))

    def send(src, dst, to, out_name, in_name):
        copy = pltpu.make_async_remote_copy(
            src_ref=src,
            dst_ref=dst,
            send_sem=send_sem.at[number(("s",) + out_name)],
            recv_sem=recv_sem.at[number(("s",) + in_name)],
            device_id=to,
            device_id_type=MESH,
        )
        copy.start()
        sent.append(copy)

    def arrived(dst, name):
        pltpu.make_async_remote_copy(
            src_ref=dst,
            dst_ref=dst,
            send_sem=send_sem.at[number(("s",) + name)],
            recv_sem=recv_sem.at[number(("s",) + name)],
            device_id=device(core=1 - core),
            device_id_type=MESH,
        ).wait_recv()

    def cols(k):
        return pl.ds(k * width, width)

    def lcols(k):
        return pl.ds(k * link, link)

    def block(ref, slot, k, count=1):
        return ref.at[pl.ds(pl.multiple_of(slot * rows, rows), count * rows), lcols(k)]

    y2, f2, core2 = 1 - y, 1 - f, 1 - core

    def begin(k):
        mine_i, mine_t = block(images, own_i, k), block(texts, own_t, k)
        send(mine_t, block(texts, own_t, k), device(f=f2), ("tf", k), ("tf", k))
        for dg in range(1, n_g):
            send(mine_i, block(images, own_i, k), device(g=(g + dg) % n_g), ("ig", dg, k), ("ig", n_g - dg, k))
        send(mine_i, block(images, own_i, k), device(y=y2), ("iy", 0, k), ("iy", 0, k))
        for dx in range(1, n_x):
            send(mine_t, block(texts, own_t, k), device(x=(x + dx) % n_x), ("tx", dx, 0, k), ("tx", n_x - dx, 0, k))
        send(mine_i, block(images, own_i, k), device(core=core2), ("ic", 0, 0, k), ("ic", 0, 0, k))

    ahead = min(AHEAD, links)
    for k in range(ahead):
        begin(k)

    def relay(k):
        for dg in range(1, n_g):
            at = block(images, image_slot(g=(g + dg) % n_g), k)
            arrived(at, ("ig", dg, k))
            send(at, at, device(y=y2), ("iy", dg, k), ("iy", dg, k))
            send(at, at, device(core=core2), ("ic", dg, 0, k), ("ic", dg, 0, k))
        at = block(texts, text_slot(f=f2), k)
        arrived(at, ("tf", k))
        for dx in range(1, n_x):
            send(at, at, device(x=(x + dx) % n_x), ("tx", dx, 1, k), ("tx", n_x - dx, 1, k))
        at = block(images, image_slot(y=y2), k)
        arrived(at, ("iy", 0, k))
        send(at, at, device(core=core2), ("ic", 0, 1, k), ("ic", 0, 1, k))

    def relay_last(k):
        for dg in range(1, n_g):
            at = block(images, image_slot(g=(g + dg) % n_g, y=y2), k)
            arrived(at, ("iy", dg, k))
            send(at, at, device(core=core2), ("ic", dg, 1, k), ("ic", dg, 1, k))

    def collect(k):
        for dx in range(1, n_x):
            for df in range(2):
                arrived(block(texts, text_slot(x=(x + dx) % n_x, f=(f + df) % 2), k), ("tx", dx, df, k))
        for dg in range(n_g):
            for dy in range(2):
                at = block(images, image_slot(g=(g + dg) % n_g, y=(y + dy) % 2, core=core2), k)
                arrived(at, ("ic", dg, dy, k))

    scale = scale_ref[0]
    n_images, n_texts = images.shape[0], texts.shape[0]
    step = min(256, n_images)
    steps = n_images // step

    def score(k):
        col = cols(k)
        hi, mid, lo = split3(texts[:, col])
        t_hi[:, col], t_mid[:, col], t_lo[...] = hi, mid, lo

        def tile(t):
            part = span(t, step)
            a_hi, a_mid, a_lo = split3(images[part, col])
            i_hi[part, col], i_mid[part, col] = a_hi, a_mid
            b_hi, b_mid, b_lo = t_hi[:, col], t_mid[:, col], t_lo[...]
            total = dot(a_lo, b_hi, NT) + dot(a_hi, b_lo, NT) + dot(a_mid, b_mid, NT)
            total = total + dot(a_mid, b_hi, NT) + dot(a_hi, b_mid, NT)
            total = total + dot(a_hi, b_hi, NT)
            if k > 0:
                total = total + scores[part, :]
            if k == chunks - 1:
                total = scale * total
            scores[part, :] = total

        tiles(steps, tile)

    for k in range(links + 2):
        if k < links:
            relay(k)
        if k + ahead < links:
            begin(k + ahead)
        if 1 <= k <= links:
            relay_last(k - 1)
        if k >= 2:
            collect(k - 2)
            if (k - 1) % ratio == 0:
                score((k - 1) // ratio - 1)

    def to_lanes(column):
        return jnp.transpose(jnp.broadcast_to(column, (column.shape[0], 128)))[0:1, :]

    def to_rows(line):
        return jnp.transpose(jnp.broadcast_to(line, (128, line.shape[1])))[:, 0:1]

    col_stats[own_t] = jnp.full((1, n_texts), -3e38, F32)

    def row_tile(t):
        part = span(t, step)
        s = scores[part, :]
        top = jnp.max(s, axis=1, keepdims=True)
        total = jnp.sum(jnp.exp(s - top), axis=1, keepdims=True)
        row_stats[own_i, :, part] = to_lanes(top + jnp.log(total))
        col_stats[own_t] = jnp.maximum(col_stats[own_t], jnp.max(s, axis=0, keepdims=True))

    tiles(steps, row_tile)
    for (dg, dy, dc), back, to in image_peers:
        here = row_stats.at[own_i]
        send(here, here, to, ("rs", dg, dy, dc), ("rs",) + back)

    col_top = col_stats[own_t]
    col_stats[own_t] = jnp.zeros((1, n_texts), F32)

    def col_tile(t):
        s = scores[span(t, step), :]
        col_stats[own_t] = col_stats[own_t] + jnp.sum(jnp.exp(s - col_top), axis=0, keepdims=True)

    tiles(steps, col_tile)
    col_stats[own_t] = col_top + jnp.log(col_stats[own_t])
    for (dx, df), back, to in text_peers:
        here = col_stats.at[own_t]
        send(here, here, to, ("cs", dx, df), ("cs",) + back)

    diagonal = scale * jnp.sum(images[own_images, :] * texts[own_texts, :])

    for (dg, dy, dc), _, _ in image_peers:
        slot = image_slot((g + dg) % n_g, (y + dy) % 2, (core + dc) % 2)
        arrived(row_stats.at[slot], ("rs", dg, dy, dc))
    for (dx, df), _, _ in text_peers:
        arrived(col_stats.at[text_slot((x + dx) % n_x, (f + df) % 2)], ("cs", dx, df))

    def merged(stats):
        every = stats[...]
        top = jnp.max(every, axis=0)
        return top + jnp.log(jnp.sum(jnp.exp(every - top[None]), axis=0))

    row_lse, col_lse = merged(row_stats), merged(col_stats)

    weighted = jnp.zeros((1, n_texts), F32)
    for t in range(steps):
        part = span(t, step)
        s = scores[part, :]
        w = 0.5 * (jnp.exp(s - to_rows(row_lse[:, t * step : (t + 1) * step])) + jnp.exp(s - col_lse))
        weighted = weighted + jnp.sum(w * s, axis=0, keepdims=True)
        w_hi[part, :], w_lo[part, :] = split2(w)
        wt_hi[:, part], wt_lo[:, part] = split2(jnp.transpose(w))

    t_step = min(256, n_texts)

    def partial_texts(k):
        col = cols(k)

        def tile(t):
            part = span(t, t_step)
            a_hi, a_lo, b_hi, b_lo = wt_hi[part, :], wt_lo[part, :], i_hi[:, col], i_mid[:, col]
            part_t[part, col] = dot(a_lo, b_hi, NN) + dot(a_hi, b_lo, NN) + dot(a_hi, b_hi, NN)

        tiles(n_texts // t_step, tile)

    def partial_images(k):
        col = cols(k)

        def tile(t):
            part = span(t, step)
            a_hi, a_lo, b_hi, b_lo = w_hi[part, :], w_lo[part, :], t_hi[:, col], t_mid[:, col]
            part_i[part, col] = dot(a_lo, b_hi, NN) + dot(a_hi, b_lo, NN) + dot(a_hi, b_hi, NN)

        tiles(steps, tile)

    def rows_of(slot, count=1):
        return pl.ds(pl.multiple_of(slot * rows, rows), count * rows)

    def send_x(k):
        for dx in range(1, n_x):
            xx = (x + dx) % n_x
            src, dst = block(part_t, xx * 2, k, 2), from_x.at[n_x - dx - 1, :, lcols(k)]
            send(src, dst, device(x=xx), ("bx", dx, k), ("bx", n_x - dx, k))

    def send_core(k):
        src, dst = block(part_i, core2 * half, k, half), from_core.at[:, lcols(k)]
        send(src, dst, device(core=core2), ("bc", k), ("bc", k))

    base = core * half

    def send_y(k):
        col = lcols(k)
        arrived(from_core.at[:, col], ("bc", k))
        away = rows_of(base + y2 * n_g, n_g)
        part_i[away, col] = part_i[away, col] + from_core[rows_of(y2 * n_g, n_g), col]
        send(part_i.at[away, col], from_y.at[:, col], device(y=y2), ("by", k), ("by", k))
        keep = rows_of(base + y * n_g, n_g)
        part_i[keep, col] = part_i[keep, col] + from_core[rows_of(y * n_g, n_g), col]

    def send_f(k):
        col = lcols(k)
        for dx in range(1, n_x):
            arrived(from_x.at[dx - 1, :, col], ("bx", dx, k))
        away, keep = rows_of(x * 2 + f2), rows_of(x * 2 + f)
        total = part_t[away, col]
        for dx in range(1, n_x):
            total = total + from_x[dx - 1, rows_of(f2), col]
        part_t[away, col] = total
        send(part_t.at[away, col], from_f.at[x, :, col], device(f=f2), ("bf", 0, k), ("bf", 0, k))
        total = part_t[keep, col]
        for dx in range(1, n_x):
            total = total + from_x[dx - 1, rows_of(f), col]
        part_t[keep, col] = total

    def send_g(k):
        col = lcols(k)
        arrived(from_y.at[:, col], ("by", k))
        for dg in range(1, n_g):
            gg = (g + dg) % n_g
            away = rows_of(base + y * n_g + gg)
            part_i[away, col] = part_i[away, col] + from_y[rows_of(gg), col]
            dst = from_g.at[n_g - dg - 1, 0, :, col]
            send(part_i.at[away, col], dst, device(g=gg), ("bg", dg, 0, k), ("bg", n_g - dg, 0, k))

    def early_f(k):
        col = lcols(k)
        for dx in range(n_x):
            xx = (x + dx) % n_x
            away = rows_of(xx * 2 + f2)
            send(part_t.at[away, col], from_f.at[xx, :, col], device(f=f2), ("bf", dx, k), ("bf", dx, k))

    def early_x(k):
        col = lcols(k)
        for dx in range(1, n_x):
            xx = (x + dx) % n_x
            away = rows_of(xx * 2 + f)
            arrived(from_f.at[xx, :, col], ("bf", dx, k))
            part_t[away, col] = part_t[away, col] + from_f[xx, :, col]
            dst = from_x.at[n_x - dx - 1, 0:rows, col]
            send(part_t.at[away, col], dst, device(x=xx), ("bx", dx, k), ("bx", n_x - dx, k))

    def early_g(k):
        col = lcols(k)
        arrived(from_core.at[:, col], ("bc", k))
        for dg in range(1, n_g):
            gg = (g + dg) % n_g
            for j in range(2):
                at = ((y + j) % 2) * n_g + gg
                away = rows_of(base + at)
                part_i[away, col] = part_i[away, col] + from_core[rows_of(at), col]
                dst = from_g.at[n_g - dg - 1, j, :, col]
                send(part_i.at[away, col], dst, device(g=gg), ("bg", dg, j, k), ("bg", n_g - dg, j, k))
        for j in range(2):
            at = ((y + j) % 2) * n_g + g
            keep = rows_of(base + at)
            part_i[keep, col] = part_i[keep, col] + from_core[rows_of(at), col]

    def early_y(k):
        col = lcols(k)
        away = rows_of(base + y2 * n_g + g)
        total = part_i[away, col]
        for dg in range(1, n_g):
            arrived(from_g.at[dg - 1, 1, :, col], ("bg", dg, 1, k))
            total = total + from_g[dg - 1, 1, :, col]
        part_i[away, col] = total
        send(part_i.at[away, col], from_y.at[0:rows, col], device(y=y2), ("by", k), ("by", k))

    early = min(EARLY, links - 1)
    for k in range(chunks):
        partial_texts(k)
        for j in range(k * ratio, (k + 1) * ratio):
            if j < early:
                early_f(j)
            else:
                send_x(j)
        if k > 0:
            partial_images(k - 1)
            for j in range((k - 1) * ratio, k * ratio):
                send_core(j)
    partial_images(chunks - 1)
    for j in range((chunks - 1) * ratio, links):
        send_core(j)
    for k in range(links):
        if k < early:
            early_g(k)
        else:
            send_y(k)

    row_lane = lax.broadcasted_iota(jnp.int32, (1, n_images), 1) // rows
    col_lane = lax.broadcasted_iota(jnp.int32, (1, n_texts), 1) // rows
    own_rows = jnp.sum(jnp.where(row_lane == own_i, row_lse, 0.0))
    own_cols = jnp.sum(jnp.where(col_lane == own_t, col_lse, 0.0))
    loss_part = 0.5 * own_rows + 0.5 * own_cols - diagonal
    scale_part = jnp.sum(weighted) - diagonal
    lane = lax.broadcasted_iota(jnp.int32, (1, 128), 1)
    totals_i[own_i] = jnp.where(lane == 0, loss_part, jnp.where(lane == 1, scale_part, 0.0))
    for (dg, dy, dc), back, to in image_peers:
        here = totals_i.at[own_i]
        send(here, here, to, ("ti", dg, dy, dc), ("ti",) + back)

    for k in range(early, links):
        send_f(k)
        if k == links - 1:
            for j in range(early):
                early_x(j)
                early_y(j)
        send_g(k)

    for (dg, dy, dc), _, _ in image_peers:
        slot = image_slot((g + dg) % n_g, (y + dy) % 2, (core + dc) % 2)
        arrived(totals_i.at[slot], ("ti", dg, dy, dc))
    totals_t[own_t] = jnp.sum(totals_i[...], axis=0)
    for (dx, df), back, to in text_peers:
        here = totals_t.at[own_t]
        send(here, here, to, ("tt", dx, df), ("tt",) + back)

    for k in [*range(early, links), *range(early)]:
        col = lcols(k)
        arrived(from_f.at[x, :, col], ("bf", 0, k))
        total = part_t[rows_of(x * 2 + f), col] + from_f[x, :, col]
        if k < early:
            for dx in range(1, n_x):
                arrived(from_x.at[dx - 1, 0:rows, col], ("bx", dx, k))
                total = total + from_x[dx - 1, 0:rows, col]
        text_grad_ref[:, col] = scale * (total - images[own_images, col])
        total = part_i[rows_of(own_i), col]
        for dg in range(1, n_g):
            arrived(from_g.at[dg - 1, 0, :, col], ("bg", dg, 0, k))
            total = total + from_g[dg - 1, 0, :, col]
        if k < early:
            arrived(from_y.at[0:rows, col], ("by", k))
            total = total + from_y[0:rows, col]
        else:
            total = total + from_y[rows_of(g), col]
        image_grad_ref[:, col] = scale * (total - texts[own_texts, col])

    for (dx, df), _, _ in text_peers:
        arrived(totals_t.at[text_slot((x + dx) % n_x, (f + df) % 2)], ("tt", dx, df))
    total = jnp.sum(totals_t[...], axis=0)
    batch = rows * n_blk * n_group
    loss_ref[0] = jnp.sum(jnp.where(lane == 0, total, 0.0)) / batch
    scale_grad_ref[0] = jnp.sum(jnp.where(lane == 1, total, 0.0)) / (scale * batch)

    for copy in sent:
        copy.wait_send()


def body(n_blk, n_group, image_feats, text_feats, logit_scale):
    rows, emb = image_feats.shape
    width = 256 if emb % 256 == 0 else emb
    n_g, n_x = n_blk // 4, n_group // 2
    n_images, n_texts = rows * n_blk, rows * n_group
    links = emb // (LINK_WIDTH if width % LINK_WIDTH == 0 else width)
    count = links * (n_g * 6 + n_x * 5 + 8) + 2 * (n_blk + n_group)
    vmem = pl.BlockSpec(memory_space=pltpu.VMEM)
    smem = pl.BlockSpec(memory_space=pltpu.SMEM)
    hbm = pl.BlockSpec(memory_space=pl.ANY)
    image_grad, text_grad, mean_loss, scale_grad = pl.pallas_call(
        functools.partial(kernel, n_blk, n_group, width),
        out_shape=(
            jax.ShapeDtypeStruct((rows, emb), F32),
            jax.ShapeDtypeStruct((rows, emb), F32),
            jax.ShapeDtypeStruct((1,), F32),
            jax.ShapeDtypeStruct((1,), F32),
        ),
        in_specs=[smem, hbm, hbm],
        out_specs=(vmem, vmem, smem, smem),
        scratch_shapes=[
            pltpu.VMEM((n_images, emb), F32),
            pltpu.VMEM((n_texts, emb), F32),
            pltpu.VMEM((n_images, n_texts), F32),
            pltpu.VMEM((n_images, emb), BF16),
            pltpu.VMEM((n_images, emb), BF16),
            pltpu.VMEM((n_texts, emb), BF16),
            pltpu.VMEM((n_texts, emb), BF16),
            pltpu.VMEM((n_texts, width), BF16),
            pltpu.VMEM((n_images, n_texts), BF16),
            pltpu.VMEM((n_images, n_texts), BF16),
            pltpu.VMEM((n_texts, n_images), BF16),
            pltpu.VMEM((n_texts, n_images), BF16),
            pltpu.VMEM((n_images, emb), F32),
            pltpu.VMEM((n_texts, emb), F32),
            pltpu.VMEM((n_images // 2, emb), F32),
            pltpu.VMEM((n_g * rows, emb), F32),
            pltpu.VMEM((max(n_g - 1, 1), 2, rows, emb), F32),
            pltpu.VMEM((max(n_x - 1, 1), 2 * rows, emb), F32),
            pltpu.VMEM((n_x, rows, emb), F32),
            pltpu.VMEM((n_blk, 1, n_images), F32),
            pltpu.VMEM((n_group, 1, n_texts), F32),
            pltpu.VMEM((n_blk, 1, 128), F32),
            pltpu.VMEM((n_group, 1, 128), F32),
            pltpu.SemaphoreType.DMA((count,)),
            pltpu.SemaphoreType.DMA((count,)),
            pltpu.SemaphoreType.DMA((2,)),
        ],
        compiler_params=pltpu.CompilerParams(
            collective_id=0, has_side_effects=True, vmem_limit_bytes=56 * 1024 * 1024
        ),
        name="contrastive",
    )(logit_scale, image_feats, text_feats)
    return image_grad, text_grad, mean_loss, scale_grad


def solution(mesh):
    return jax.shard_map(
        functools.partial(body, mesh.shape["blk"], mesh.shape["group"]),
        mesh=mesh,
        in_specs=(P(("blk", "group"), None), P(("blk", "group"), None), P()),
        out_specs=(P(("blk", "group"), None), P(("blk", "group"), None), P(), P()),
        check_vma=False,
    )
```

```python
import functools

import jax
import jax.numpy as jnp
from jax import lax
from jax.experimental import pallas as pl
from jax.experimental.pallas import tpu as pltpu
from jax.sharding import PartitionSpec as P

F32 = jnp.float32
BF16 = jnp.bfloat16
MESH = pl.DeviceIdType.MESH
NT = (((1,), (1,)), ((), ()))
NN = (((1,), (0,)), ((), ()))


LINK_WIDTH = 256
AHEAD = 3
EARLY = 1


def dot(a, b, dims):
    return lax.dot_general(a, b, dims, preferred_element_type=F32)


def split2(x):
    hi = x.astype(BF16)
    return hi, (x - hi.astype(F32)).astype(BF16)


def split3(x):
    hi = x.astype(BF16)
    rest = x - hi.astype(F32)
    mid = rest.astype(BF16)
    return hi, mid, (rest - mid.astype(F32)).astype(BF16)


def tiles(count, fn):
    if count <= 2:
        for t in range(count):
            fn(t)
    else:
        lax.fori_loop(0, count, lambda t, c: (fn(t), c)[1], 0)


def span(t, step):
    start = t * step
    return pl.ds(start if isinstance(start, int) else pl.multiple_of(start, step), step)


def kernel(
    n_blk,
    n_group,
    width,
    scale_ref,
    image_ref,
    text_ref,
    image_grad_ref,
    text_grad_ref,
    loss_ref,
    scale_grad_ref,
    images,
    texts,
    scores,
    i_hi,
    i_mid,
    t_hi,
    t_mid,
    t_lo,
    w_hi,
    w_lo,
    wt_hi,
    wt_lo,
    part_i,
    part_t,
    from_core,
    from_y,
    from_g,
    from_x,
    from_f,
    row_stats,
    col_stats,
    totals_i,
    totals_t,
    send_sem,
    recv_sem,
    load_sem,
):
    rows, emb = image_ref.shape
    chunks = emb // width
    link = LINK_WIDTH if width % LINK_WIDTH == 0 else width
    links, ratio = emb // link, width // link
    n_g, n_x = n_blk // 4, n_group // 2
    half = n_blk // 2
    blk, group = lax.axis_index("blk"), lax.axis_index("group")
    f, r = blk // half, blk % half
    g, y = r // 2, r % 2
    x, core = group // 2, group % 2

    def device(f=f, g=g, y=y, x=x, core=core):
        return (f * half + g * 2 + y, x * 2 + core)

    def image_slot(g=g, y=y, core=core):
        return core * half + y * n_g + g

    def text_slot(x=x, f=f):
        return x * 2 + f

    image_peers = []
    for dc in range(2):
        for dy in range(2):
            for dg in range(n_g):
                if dc or dy or dg:
                    to = device(g=(g + dg) % n_g, y=(y + dy) % 2, core=(core + dc) % 2)
                    image_peers.append(((dg, dy, dc), ((n_g - dg) % n_g, dy, dc), to))
    text_peers = []
    for dx in range(n_x):
        for df in range(2):
            if dx or df:
                to = device(x=(x + dx) % n_x, f=(f + df) % 2)
                text_peers.append(((dx, df), ((n_x - dx) % n_x, df), to))

    own_i, own_t = image_slot(), text_slot()
    own_images = pl.ds(pl.multiple_of(own_i * rows, rows), rows)
    own_texts = pl.ds(pl.multiple_of(own_t * rows, rows), rows)
    loads = [
        pltpu.make_async_copy(image_ref, images.at[own_images], load_sem.at[0]),
        pltpu.make_async_copy(text_ref, texts.at[own_texts], load_sem.at[1]),
    ]
    barrier = pltpu.get_barrier_semaphore()
    for _, _, to in text_peers + image_peers:
        pl.semaphore_signal(barrier, inc=1, device_id=to, device_id_type=MESH)
    for load in loads:
        load.start()
    pl.semaphore_wait(barrier, len(image_peers) + len(text_peers))
    for load in loads:
        load.wait()

    numbers = {}
    sent = []

    def number(name):
        return numbers.setdefault(name, len(numbers))

    def send(src, dst, to, out_name, in_name):
        copy = pltpu.make_async_remote_copy(
            src_ref=src,
            dst_ref=dst,
            send_sem=send_sem.at[number(("s",) + out_name)],
            recv_sem=recv_sem.at[number(("s",) + in_name)],
            device_id=to,
            device_id_type=MESH,
        )
        copy.start()
        sent.append(copy)

    def arrived(dst, name):
        pltpu.make_async_remote_copy(
            src_ref=dst,
            dst_ref=dst,
            send_sem=send_sem.at[number(("s",) + name)],
            recv_sem=recv_sem.at[number(("s",) + name)],
            device_id=device(core=1 - core),
            device_id_type=MESH,
        ).wait_recv()

    def cols(k):
        return pl.ds(k * width, width)

    def lcols(k):
        return pl.ds(k * link, link)

    def block(ref, slot, k, count=1):
        return ref.at[pl.ds(pl.multiple_of(slot * rows, rows), count * rows), lcols(k)]

    y2, f2, core2 = 1 - y, 1 - f, 1 - core

    def begin(k):
        mine_i, mine_t = block(images, own_i, k), block(texts, own_t, k)
        send(mine_t, block(texts, own_t, k), device(f=f2), ("tf", k), ("tf", k))
        for dg in range(1, n_g):
            send(mine_i, block(images, own_i, k), device(g=(g + dg) % n_g), ("ig", dg, k), ("ig", n_g - dg, k))
        send(mine_i, block(images, own_i, k), device(y=y2), ("iy", 0, k), ("iy", 0, k))
        for dx in range(1, n_x):
            send(mine_t, block(texts, own_t, k), device(x=(x + dx) % n_x), ("tx", dx, 0, k), ("tx", n_x - dx, 0, k))
        send(mine_i, block(images, own_i, k), device(core=core2), ("ic", 0, 0, k), ("ic", 0, 0, k))

    ahead = min(AHEAD, links)
    for k in range(ahead):
        begin(k)

    def relay(k):
        at = block(images, image_slot(y=y2), k)
        arrived(at, ("iy", 0, k))
        send(at, at, device(core=core2), ("ic", 0, 1, k), ("ic", 0, 1, k))
        for dg in range(1, n_g):
            at = block(images, image_slot(g=(g + dg) % n_g), k)
            arrived(at, ("ig", dg, k))
            send(at, at, device(y=y2), ("iy", dg, k), ("iy", dg, k))
            send(at, at, device(core=core2), ("ic", dg, 0, k), ("ic", dg, 0, k))
        at = block(texts, text_slot(f=f2), k)
        arrived(at, ("tf", k))
        for dx in range(1, n_x):
            send(at, at, device(x=(x + dx) % n_x), ("tx", dx, 1, k), ("tx", n_x - dx, 1, k))

    def relay_last(k):
        for dg in range(1, n_g):
            at = block(images, image_slot(g=(g + dg) % n_g, y=y2), k)
            arrived(at, ("iy", dg, k))
            send(at, at, device(core=core2), ("ic", dg, 1, k), ("ic", dg, 1, k))

    def collect(k):
        for dx in range(1, n_x):
            for df in range(2):
                arrived(block(texts, text_slot(x=(x + dx) % n_x, f=(f + df) % 2), k), ("tx", dx, df, k))
        for dg in range(n_g):
            for dy in range(2):
                at = block(images, image_slot(g=(g + dg) % n_g, y=(y + dy) % 2, core=core2), k)
                arrived(at, ("ic", dg, dy, k))

    scale = scale_ref[0]
    n_images, n_texts = images.shape[0], texts.shape[0]
    step = min(256, n_images)
    steps = n_images // step

    def score(k):
        col = cols(k)
        hi, mid, lo = split3(texts[:, col])
        t_hi[:, col], t_mid[:, col], t_lo[...] = hi, mid, lo

        def tile(t):
            part = span(t, step)
            a_hi, a_mid, a_lo = split3(images[part, col])
            i_hi[part, col], i_mid[part, col] = a_hi, a_mid
            b_hi, b_mid, b_lo = t_hi[:, col], t_mid[:, col], t_lo[...]
            total = dot(a_lo, b_hi, NT) + dot(a_hi, b_lo, NT) + dot(a_mid, b_mid, NT)
            total = total + dot(a_mid, b_hi, NT) + dot(a_hi, b_mid, NT)
            total = total + dot(a_hi, b_hi, NT)
            if k > 0:
                total = total + scores[part, :]
            if k == chunks - 1:
                total = scale * total
            scores[part, :] = total

        tiles(steps, tile)

    for k in range(links + 2):
        if k < links:
            relay(k)
        if k + ahead < links:
            begin(k + ahead)
        if 1 <= k <= links:
            relay_last(k - 1)
        if k >= 2:
            collect(k - 2)
            if (k - 1) % ratio == 0:
                score((k - 1) // ratio - 1)

    def to_lanes(column):
        return jnp.transpose(jnp.broadcast_to(column, (column.shape[0], 128)))[0:1, :]

    def to_rows(line):
        return jnp.transpose(jnp.broadcast_to(line, (128, line.shape[1])))[:, 0:1]

    col_stats[own_t] = jnp.full((1, n_texts), -3e38, F32)

    def row_tile(t):
        part = span(t, step)
        s = scores[part, :]
        top = jnp.max(s, axis=1, keepdims=True)
        total = jnp.sum(jnp.exp(s - top), axis=1, keepdims=True)
        row_stats[own_i, :, part] = to_lanes(top + jnp.log(total))
        col_stats[own_t] = jnp.maximum(col_stats[own_t], jnp.max(s, axis=0, keepdims=True))

    tiles(steps, row_tile)
    for (dg, dy, dc), back, to in image_peers:
        here = row_stats.at[own_i]
        send(here, here, to, ("rs", dg, dy, dc), ("rs",) + back)

    col_top = col_stats[own_t]
    col_stats[own_t] = jnp.zeros((1, n_texts), F32)

    def col_tile(t):
        s = scores[span(t, step), :]
        col_stats[own_t] = col_stats[own_t] + jnp.sum(jnp.exp(s - col_top), axis=0, keepdims=True)

    tiles(steps, col_tile)
    col_stats[own_t] = col_top + jnp.log(col_stats[own_t])
    for (dx, df), back, to in text_peers:
        here = col_stats.at[own_t]
        send(here, here, to, ("cs", dx, df), ("cs",) + back)

    diagonal = scale * jnp.sum(images[own_images, :] * texts[own_texts, :])

    for (dg, dy, dc), _, _ in image_peers:
        slot = image_slot((g + dg) % n_g, (y + dy) % 2, (core + dc) % 2)
        arrived(row_stats.at[slot], ("rs", dg, dy, dc))
    for (dx, df), _, _ in text_peers:
        arrived(col_stats.at[text_slot((x + dx) % n_x, (f + df) % 2)], ("cs", dx, df))

    def merged(stats):
        every = stats[...]
        top = jnp.max(every, axis=0)
        return top + jnp.log(jnp.sum(jnp.exp(every - top[None]), axis=0))

    row_lse, col_lse = merged(row_stats), merged(col_stats)

    weighted = jnp.zeros((1, n_texts), F32)
    for t in range(steps):
        part = span(t, step)
        s = scores[part, :]
        w = 0.5 * (jnp.exp(s - to_rows(row_lse[:, t * step : (t + 1) * step])) + jnp.exp(s - col_lse))
        weighted = weighted + jnp.sum(w * s, axis=0, keepdims=True)
        w_hi[part, :], w_lo[part, :] = split2(w)
        wt_hi[:, part], wt_lo[:, part] = split2(jnp.transpose(w))

    t_step = min(256, n_texts)

    def partial_texts(k):
        col = cols(k)

        def tile(t):
            part = span(t, t_step)
            a_hi, a_lo, b_hi, b_lo = wt_hi[part, :], wt_lo[part, :], i_hi[:, col], i_mid[:, col]
            part_t[part, col] = dot(a_lo, b_hi, NN) + dot(a_hi, b_lo, NN) + dot(a_hi, b_hi, NN)

        tiles(n_texts // t_step, tile)

    def partial_images(k):
        col = cols(k)

        def tile(t):
            part = span(t, step)
            a_hi, a_lo, b_hi, b_lo = w_hi[part, :], w_lo[part, :], t_hi[:, col], t_mid[:, col]
            part_i[part, col] = dot(a_lo, b_hi, NN) + dot(a_hi, b_lo, NN) + dot(a_hi, b_hi, NN)

        tiles(steps, tile)

    def rows_of(slot, count=1):
        return pl.ds(pl.multiple_of(slot * rows, rows), count * rows)

    def send_x(k):
        for dx in range(1, n_x):
            xx = (x + dx) % n_x
            src, dst = block(part_t, xx * 2, k, 2), from_x.at[n_x - dx - 1, :, lcols(k)]
            send(src, dst, device(x=xx), ("bx", dx, k), ("bx", n_x - dx, k))

    def send_core(k):
        src, dst = block(part_i, core2 * half, k, half), from_core.at[:, lcols(k)]
        send(src, dst, device(core=core2), ("bc", k), ("bc", k))

    base = core * half

    def send_y(k):
        col = lcols(k)
        arrived(from_core.at[:, col], ("bc", k))
        away = rows_of(base + y2 * n_g, n_g)
        part_i[away, col] = part_i[away, col] + from_core[rows_of(y2 * n_g, n_g), col]
        send(part_i.at[away, col], from_y.at[:, col], device(y=y2), ("by", k), ("by", k))
        keep = rows_of(base + y * n_g, n_g)
        part_i[keep, col] = part_i[keep, col] + from_core[rows_of(y * n_g, n_g), col]

    def send_f(k):
        col = lcols(k)
        for dx in range(1, n_x):
            arrived(from_x.at[dx - 1, :, col], ("bx", dx, k))
        away, keep = rows_of(x * 2 + f2), rows_of(x * 2 + f)
        total = part_t[away, col]
        for dx in range(1, n_x):
            total = total + from_x[dx - 1, rows_of(f2), col]
        part_t[away, col] = total
        send(part_t.at[away, col], from_f.at[x, :, col], device(f=f2), ("bf", 0, k), ("bf", 0, k))
        total = part_t[keep, col]
        for dx in range(1, n_x):
            total = total + from_x[dx - 1, rows_of(f), col]
        part_t[keep, col] = total

    def send_g(k):
        col = lcols(k)
        arrived(from_y.at[:, col], ("by", k))
        for dg in range(1, n_g):
            gg = (g + dg) % n_g
            away = rows_of(base + y * n_g + gg)
            part_i[away, col] = part_i[away, col] + from_y[rows_of(gg), col]
            dst = from_g.at[n_g - dg - 1, 0, :, col]
            send(part_i.at[away, col], dst, device(g=gg), ("bg", dg, 0, k), ("bg", n_g - dg, 0, k))

    def early_f(k):
        col = lcols(k)
        for dx in range(n_x):
            xx = (x + dx) % n_x
            away = rows_of(xx * 2 + f2)
            send(part_t.at[away, col], from_f.at[xx, :, col], device(f=f2), ("bf", dx, k), ("bf", dx, k))

    def early_x(k):
        col = lcols(k)
        for dx in range(1, n_x):
            xx = (x + dx) % n_x
            away = rows_of(xx * 2 + f)
            arrived(from_f.at[xx, :, col], ("bf", dx, k))
            part_t[away, col] = part_t[away, col] + from_f[xx, :, col]
            dst = from_x.at[n_x - dx - 1, 0:rows, col]
            send(part_t.at[away, col], dst, device(x=xx), ("bx", dx, k), ("bx", n_x - dx, k))

    def early_g(k):
        col = lcols(k)
        arrived(from_core.at[:, col], ("bc", k))
        for dg in range(1, n_g):
            gg = (g + dg) % n_g
            for j in range(2):
                at = ((y + j) % 2) * n_g + gg
                away = rows_of(base + at)
                part_i[away, col] = part_i[away, col] + from_core[rows_of(at), col]
                dst = from_g.at[n_g - dg - 1, j, :, col]
                send(part_i.at[away, col], dst, device(g=gg), ("bg", dg, j, k), ("bg", n_g - dg, j, k))
        for j in range(2):
            at = ((y + j) % 2) * n_g + g
            keep = rows_of(base + at)
            part_i[keep, col] = part_i[keep, col] + from_core[rows_of(at), col]

    def early_y(k):
        col = lcols(k)
        away = rows_of(base + y2 * n_g + g)
        total = part_i[away, col]
        for dg in range(1, n_g):
            arrived(from_g.at[dg - 1, 1, :, col], ("bg", dg, 1, k))
            total = total + from_g[dg - 1, 1, :, col]
        part_i[away, col] = total
        send(part_i.at[away, col], from_y.at[0:rows, col], device(y=y2), ("by", k), ("by", k))

    early = min(EARLY, links - 1)
    for k in range(chunks):
        partial_texts(k)
        for j in range(k * ratio, (k + 1) * ratio):
            if j < early:
                early_f(j)
            else:
                send_x(j)
        if k > 0:
            partial_images(k - 1)
            for j in range((k - 1) * ratio, k * ratio):
                send_core(j)
    partial_images(chunks - 1)
    for j in range((chunks - 1) * ratio, links):
        send_core(j)
    for k in range(links):
        if k < early:
            early_g(k)
        else:
            send_y(k)

    row_lane = lax.broadcasted_iota(jnp.int32, (1, n_images), 1) // rows
    col_lane = lax.broadcasted_iota(jnp.int32, (1, n_texts), 1) // rows
    own_rows = jnp.sum(jnp.where(row_lane == own_i, row_lse, 0.0))
    own_cols = jnp.sum(jnp.where(col_lane == own_t, col_lse, 0.0))
    loss_part = 0.5 * own_rows + 0.5 * own_cols - diagonal
    scale_part = jnp.sum(weighted) - diagonal
    lane = lax.broadcasted_iota(jnp.int32, (1, 128), 1)
    totals_i[own_i] = jnp.where(lane == 0, loss_part, jnp.where(lane == 1, scale_part, 0.0))
    for (dg, dy, dc), back, to in image_peers:
        here = totals_i.at[own_i]
        send(here, here, to, ("ti", dg, dy, dc), ("ti",) + back)

    for k in range(early, links):
        send_f(k)
        if k == links - 1:
            for j in range(early):
                early_x(j)
                early_y(j)
        send_g(k)

    for (dg, dy, dc), _, _ in image_peers:
        slot = image_slot((g + dg) % n_g, (y + dy) % 2, (core + dc) % 2)
        arrived(totals_i.at[slot], ("ti", dg, dy, dc))
    totals_t[own_t] = jnp.sum(totals_i[...], axis=0)
    for (dx, df), back, to in text_peers:
        here = totals_t.at[own_t]
        send(here, here, to, ("tt", dx, df), ("tt",) + back)

    for k in [*range(early, links), *range(early)]:
        col = lcols(k)
        arrived(from_f.at[x, :, col], ("bf", 0, k))
        total = part_t[rows_of(x * 2 + f), col] + from_f[x, :, col]
        if k < early:
            for dx in range(1, n_x):
                arrived(from_x.at[dx - 1, 0:rows, col], ("bx", dx, k))
                total = total + from_x[dx - 1, 0:rows, col]
        text_grad_ref[:, col] = scale * (total - images[own_images, col])
        total = part_i[rows_of(own_i), col]
        for dg in range(1, n_g):
            arrived(from_g.at[dg - 1, 0, :, col], ("bg", dg, 0, k))
            total = total + from_g[dg - 1, 0, :, col]
        if k < early:
            arrived(from_y.at[0:rows, col], ("by", k))
            total = total + from_y[0:rows, col]
        else:
            total = total + from_y[rows_of(g), col]
        image_grad_ref[:, col] = scale * (total - texts[own_texts, col])

    for (dx, df), _, _ in text_peers:
        arrived(totals_t.at[text_slot((x + dx) % n_x, (f + df) % 2)], ("tt", dx, df))
    total = jnp.sum(totals_t[...], axis=0)
    batch = rows * n_blk * n_group
    loss_ref[0] = jnp.sum(jnp.where(lane == 0, total, 0.0)) / batch
    scale_grad_ref[0] = jnp.sum(jnp.where(lane == 1, total, 0.0)) / (scale * batch)

    for copy in sent:
        copy.wait_send()


def body(n_blk, n_group, image_feats, text_feats, logit_scale):
    rows, emb = image_feats.shape
    width = 256 if emb % 256 == 0 else emb
    n_g, n_x = n_blk // 4, n_group // 2
    n_images, n_texts = rows * n_blk, rows * n_group
    links = emb // (LINK_WIDTH if width % LINK_WIDTH == 0 else width)
    count = links * (n_g * 6 + n_x * 5 + 8) + 2 * (n_blk + n_group)
    vmem = pl.BlockSpec(memory_space=pltpu.VMEM)
    smem = pl.BlockSpec(memory_space=pltpu.SMEM)
    hbm = pl.BlockSpec(memory_space=pl.ANY)
    image_grad, text_grad, mean_loss, scale_grad = pl.pallas_call(
        functools.partial(kernel, n_blk, n_group, width),
        out_shape=(
            jax.ShapeDtypeStruct((rows, emb), F32),
            jax.ShapeDtypeStruct((rows, emb), F32),
            jax.ShapeDtypeStruct((1,), F32),
            jax.ShapeDtypeStruct((1,), F32),
        ),
        in_specs=[smem, hbm, hbm],
        out_specs=(vmem, vmem, smem, smem),
        scratch_shapes=[
            pltpu.VMEM((n_images, emb), F32),
            pltpu.VMEM((n_texts, emb), F32),
            pltpu.VMEM((n_images, n_texts), F32),
            pltpu.VMEM((n_images, emb), BF16),
            pltpu.VMEM((n_images, emb), BF16),
            pltpu.VMEM((n_texts, emb), BF16),
            pltpu.VMEM((n_texts, emb), BF16),
            pltpu.VMEM((n_texts, width), BF16),
            pltpu.VMEM((n_images, n_texts), BF16),
            pltpu.VMEM((n_images, n_texts), BF16),
            pltpu.VMEM((n_texts, n_images), BF16),
            pltpu.VMEM((n_texts, n_images), BF16),
            pltpu.VMEM((n_images, emb), F32),
            pltpu.VMEM((n_texts, emb), F32),
            pltpu.VMEM((n_images // 2, emb), F32),
            pltpu.VMEM((n_g * rows, emb), F32),
            pltpu.VMEM((max(n_g - 1, 1), 2, rows, emb), F32),
            pltpu.VMEM((max(n_x - 1, 1), 2 * rows, emb), F32),
            pltpu.VMEM((n_x, rows, emb), F32),
            pltpu.VMEM((n_blk, 1, n_images), F32),
            pltpu.VMEM((n_group, 1, n_texts), F32),
            pltpu.VMEM((n_blk, 1, 128), F32),
            pltpu.VMEM((n_group, 1, 128), F32),
            pltpu.SemaphoreType.DMA((count,)),
            pltpu.SemaphoreType.DMA((count,)),
            pltpu.SemaphoreType.DMA((2,)),
        ],
        compiler_params=pltpu.CompilerParams(
            collective_id=0, has_side_effects=True, vmem_limit_bytes=56 * 1024 * 1024
        ),
        name="contrastive",
    )(logit_scale, image_feats, text_feats)
    return image_grad, text_grad, mean_loss, scale_grad


def solution(mesh):
    return jax.shard_map(
        functools.partial(body, mesh.shape["blk"], mesh.shape["group"]),
        mesh=mesh,
        in_specs=(P(("blk", "group"), None), P(("blk", "group"), None), P()),
        out_specs=(P(("blk", "group"), None), P(("blk", "group"), None), P(), P()),
        check_vma=False,
    )
```
